32 devices in a mesh: seq: 8 (over z, x), tp: 4 (over y, core).
Axes of the slice: x: 2, y: 2, z: 4, core: 2. Of those that a mesh axis runs over, the one named last changes fastest.
Arguments:
- tokens: bfloat16 [8192, 2048], P('seq', 'tp'), may hold values from -6 to 6
- w_inner: bfloat16 [2048, 2, 4096], P('seq', None, 'tp'), may hold values from -0.125 to 0.125
- w_states: bfloat16 [2048, 256], P('seq'), may hold values from -0.125 to 0.125
- w_step: bfloat16 [2048, 64], P('seq', 'tp'), may hold values from -0.125 to 0.125
- conv_inner: float32 [4, 4096], P(None, 'tp'), may hold values from -3 to 3
- conv_states: float32 [4, 256], replicated, may hold values from -3 to 3
- decay_rate: float32 [64], P('tp'), may hold values from 0 to 1, as said below
- step_bias: float32 [64], P('tp'), may hold values from -1 to 0.5
- skip_gain: float32 [64], P('tp'), may hold values from 0.5 to 1.5
- norm_gain: float32 [4096], P('tp'), may hold values from 0.5 to 1.5
- w_output: bfloat16 [4096, 2048], P('tp', 'seq'), may hold values from -0.09375 to 0.09375
- block_owner: int32 [32], replicated, may hold values from 0 to 4, as said below
- lengths: int32 [5], replicated, may hold values from 1 to 4096, as said below
Outputs:
- mixed: bfloat16 [8192, 2048], P('seq', 'tp')
The draws below stay inside these ranges and needn't reach their ends.
Inputs may be any that keep to these rules, and one draw needn't show every extreme that they name: `block_owner`: each prompt's blocks are consecutive, prompt r has ceil(lengths[r] / 256) of them, and the prompts follow one another in an order drawn afresh; one prompt has 16 blocks and is neither the first nor the last in that order. `lengths`: one prompt has exactly 4096 tokens. `decay_rate`: Positive.
All inputs are finite; a program needn't handle non-finite values.
Results may differ from the reference program's by a relative error of at most 0.0075.
Values may be sent and summed in bfloat16 or wider, within the bound.
A program may use at most 64 MiB of HBM per device.

```python
import math
import jax
import jax.numpy as jnp
from jax import lax

D = 2048
HEADS = 64
HDIM = 64
INNER = 4096
STATE = 128
KCONV = 4
BLOCK = 256
NBLOCK = 32
TOKENS = 8192
REQ = 5
MAXBLK = 16


def request_plan(key):
    base_key = jax.random.fold_in(key, 17)
    key_long, key_pick, key_order, key_tail, key_place = jax.random.split(base_key, 5)
    longest = jax.random.randint(key_long, (), 0, REQ)
    spare_blocks = NBLOCK - MAXBLK - (REQ - 1)
    picked = jax.random.randint(key_pick, (spare_blocks,), 0, REQ - 1)
    picked = picked + (picked >= longest).astype(jnp.int32)
    request_ids = jnp.arange(REQ, dtype=jnp.int32)
    counts = 1 + jnp.sum((picked[:, None] == request_ids[None, :]).astype(jnp.int32), axis=0)
    counts = jnp.where(request_ids == longest, MAXBLK, counts)
    shuffled = jax.random.permutation(key_order, REQ).astype(jnp.int32)
    place_long = jax.random.randint(key_place, (), 1, REQ - 1)
    where_long = jnp.sum(jnp.where(shuffled == longest, request_ids, 0))
    moved = shuffled[place_long]
    request_order = jnp.where(request_ids == place_long, longest, jnp.where(request_ids == where_long, moved, shuffled))
    order_ends = jnp.cumsum(counts[request_order])
    block_ids = jnp.arange(NBLOCK, dtype=jnp.int32)
    placed = jnp.sum((order_ends[None, :] <= block_ids[:, None]).astype(jnp.int32), axis=1)
    owners = request_order[placed].astype(jnp.int32)
    tail_lengths = jax.random.randint(key_tail, (REQ,), 1, BLOCK + 1)
    tail_lengths = jnp.where(request_ids == longest, BLOCK, tail_lengths)
    lengths = (counts - 1) * BLOCK + tail_lengths
    return (owners, lengths.astype(jnp.int32))


def draw_block_owner(key, part):
    return request_plan(key)[0]


def draw_lengths(key, part):
    return request_plan(key)[1]


def draw_decay_rate(key, part):
    key_kind, key_slow, key_fast = jax.random.split(jax.random.fold_in(key, 29), 3)
    fast_heads = jax.random.randint(key_kind, (HEADS,), 0, 2) == 1
    chain_span = float(MAXBLK * BLOCK)
    slow_rates = jnp.exp(jax.random.uniform(key_slow, (HEADS,), jnp.float32, math.log(0.2), math.log(2.0))) / chain_span
    fast_rates = jnp.exp(jax.random.uniform(key_fast, (HEADS,), jnp.float32, math.log(0.03), math.log(0.05)))
    return jnp.where(fast_heads, fast_rates, slow_rates).astype(jnp.float32)


def levels(own_key, dims, cuts, smallest, top_value):
    gain, own = 1.0, jax.random.fold_in(own_key, 6)
    for dim, parts in cuts:
        heights = jnp.exp(jax.random.uniform(jax.random.fold_in(own, dim), (parts,), jnp.float32, smallest / len(cuts), top_value / len(cuts)))
        gain = gain * jnp.repeat(heights, dims[dim] // parts).reshape([-1 if axis == dim else 1 for axis in range(len(dims))])
    return gain


def normal_values(rng, shape, width, most, cuts=(), kind=jnp.bfloat16):
    factor_of = levels(rng, shape, cuts, -0.22, 0.18) if cuts else 1.0
    result = jax.random.normal(rng, shape, jnp.float32) * width * factor_of
    return jnp.minimum(jnp.maximum(result, -most), most).astype(kind)


def setup_inputs(seed: int = 0) -> dict:
    key_list = jax.random.split(jax.random.key(seed), 14)
    tokens = normal_values(key_list[0], (TOKENS, D), 1.0, 6.0, ((0, 8), (1, 4)))
    w_inner = normal_values(key_list[1], (D, 2, INNER), D ** -0.5, 0.125, ((0, 8), (2, 4)))
    w_states = normal_values(key_list[2], (D, 2 * STATE), D ** -0.5, 0.125, ((0, 8),))
    w_step = normal_values(key_list[3], (D, HEADS), D ** -0.5, 0.125, ((0, 8), (1, 4)))
    conv_inner = normal_values(key_list[4], (KCONV, INNER), KCONV ** -0.5, 3.0, ((1, 4),), jnp.float32)
    conv_states = normal_values(key_list[5], (KCONV, 2 * STATE), KCONV ** -0.5, 3.0, (), jnp.float32)
    decay_rate = draw_decay_rate(jax.random.fold_in(key_list[13], 71), 0)
    step_bias = jnp.clip(-1.0 + 1.5 * jax.random.uniform(key_list[7], (HEADS,), jnp.float32) ** levels(key_list[7], (HEADS,), ((0, 4),), -0.2, 0.2), -1.0, 0.5)
    skip_gain = jnp.clip(0.5 + 1.0 * jax.random.uniform(key_list[8], (HEADS,), jnp.float32) ** levels(key_list[8], (HEADS,), ((0, 4),), -0.2, 0.2), 0.5, 1.5)
    norm_gain = jnp.clip(0.5 + 1.0 * jax.random.uniform(key_list[9], (INNER,), jnp.float32) ** levels(key_list[9], (INNER,), ((0, 4),), -0.2, 0.2), 0.5, 1.5)
    w_output = normal_values(key_list[10], (INNER, D), INNER ** -0.5, 0.09375, ((0, 4), (1, 8)))
    block_owner = draw_block_owner(jax.random.fold_in(key_list[13], 71), 0)
    lengths = draw_lengths(jax.random.fold_in(key_list[13], 71), 0)
    return dict(tokens=tokens, w_inner=w_inner, w_states=w_states, w_step=w_step, conv_inner=conv_inner, conv_states=conv_states, decay_rate=decay_rate, step_bias=step_bias, skip_gain=skip_gain, norm_gain=norm_gain, w_output=w_output, block_owner=block_owner, lengths=lengths)


best_precision = lax.Precision.HIGHEST

def to_half(values):
    return lax.optimization_barrier(values.astype(jnp.bfloat16)).astype(jnp.float32)

def block_tables(block_owner, lengths):
    block_ids = jnp.arange(NBLOCK, dtype=jnp.int32)
    same_owner = block_owner[:, None] == block_owner[None, :]
    first_block = lax.optimization_barrier(jnp.min(jnp.where(same_owner, block_ids[None, :], NBLOCK), axis=1))
    starting = first_block == block_ids
    request_ids = jnp.arange(REQ, dtype=jnp.int32)
    own_length = lax.optimization_barrier(jnp.sum(jnp.where(block_owner[:, None] == request_ids[None, :], lengths[None, :], 0), axis=1))
    valid_rows = jnp.clip(own_length - (block_ids - first_block) * BLOCK, 0, BLOCK)
    return (starting, valid_rows)

def convolve(values, weights, in_block, carry_on):
    widened = values.astype(jnp.float32)
    total = jnp.zeros(values.shape, jnp.float32)
    for offset in range(KCONV):
        shifted = jnp.pad(widened, ((offset, 0), (0, 0)))[:values.shape[0]]
        keeping = (in_block >= offset) | carry_on
        total = total + jnp.where(keeping[:, None], shifted, 0.0) * weights[offset]
    return jax.nn.silu(total).astype(jnp.bfloat16)

def block_step(previous, inputs):
    x_block, b_block, c_block, log_block, step_block, starting = inputs
    cumulative = jnp.cumsum(log_block, axis=0)
    causal = jnp.arange(BLOCK)[:, None] >= jnp.arange(BLOCK)[None, :]
    spread = cumulative[:, None, :] - cumulative[None, :, :]
    decays = jnp.exp(jnp.where(causal[:, :, None], spread, -jnp.inf))
    intersection = jnp.einsum('in,jn->ij', c_block, b_block, precision=best_precision)
    mixing = to_half(decays * intersection[:, :, None] * step_block[None, :, :])
    y_inner = jnp.einsum('ijh,jhp->ihp', mixing, x_block, precision=best_precision)
    incoming = previous * jnp.where(starting, 0.0, 1.0)
    final_log = cumulative[-1]
    y_carry = jnp.exp(cumulative)[:, :, None] * jnp.einsum('in,hnp->ihp', c_block, to_half(incoming), precision=best_precision)
    tail_weight = jnp.exp(final_log[None, :] - cumulative) * step_block
    weighted_b = to_half(tail_weight[:, :, None] * b_block[:, None, :])
    fresh = jnp.einsum('jhn,jhp->hnp', weighted_b, x_block, precision=best_precision)
    state = jnp.exp(final_log)[:, None, None] * incoming + fresh
    return (state, y_inner + y_carry)

def reference(tokens, w_inner, w_states, w_step, conv_inner, conv_states, decay_rate, step_bias, skip_gain, norm_gain, w_output, block_owner, lengths):
    starting, valid_rows = block_tables(block_owner, lengths)
    projected = jnp.dot(tokens, w_inner.reshape(D, 2 * INNER), preferred_element_type=jnp.float32).astype(jnp.bfloat16)
    gate_in = projected[:, :INNER]
    x_in = projected[:, INNER:]
    bc_in = jnp.dot(tokens, w_states, preferred_element_type=jnp.float32).astype(jnp.bfloat16)
    step_raw = jnp.dot(tokens, w_step, preferred_element_type=jnp.float32).astype(jnp.bfloat16)
    positions = jnp.arange(TOKENS, dtype=jnp.int32)
    in_block = positions % BLOCK
    block_of = positions // BLOCK
    carry_on = jnp.logical_not(starting[block_of])
    x_conv = convolve(x_in, conv_inner, in_block, carry_on)
    bc_conv = convolve(bc_in, conv_states, in_block, carry_on)
    step_size = jax.nn.softplus(step_raw.astype(jnp.float32) + step_bias)
    log_decay = -decay_rate * step_size
    x_heads = x_conv.astype(jnp.float32).reshape(NBLOCK, BLOCK, HEADS, HDIM)
    b_rows = bc_conv[:, :STATE].astype(jnp.float32).reshape(NBLOCK, BLOCK, STATE)
    c_rows = bc_conv[:, STATE:].astype(jnp.float32).reshape(NBLOCK, BLOCK, STATE)
    initial = jnp.zeros((HEADS, STATE, HDIM), jnp.float32)
    _, y_blocks = lax.scan(block_step, initial, (x_heads, b_rows, c_rows, log_decay.reshape(NBLOCK, BLOCK, HEADS), step_size.reshape(NBLOCK, BLOCK, HEADS), starting))
    y_total = y_blocks.reshape(TOKENS, INNER) + jnp.repeat(skip_gain, HDIM)[None, :] * x_conv.astype(jnp.float32)
    gated = y_total * jax.nn.silu(gate_in.astype(jnp.float32))
    square_mean = lax.optimization_barrier(jnp.sum(gated * gated, axis=1)) / INNER
    normed = (gated * lax.rsqrt(square_mean + 1e-05)[:, None] * norm_gain).astype(jnp.bfloat16)
    mixed = jnp.dot(normed, w_output, preferred_element_type=jnp.float32)
    live = in_block < valid_rows[block_of]
    return jnp.where(live[:, None], mixed, 0.0).astype(jnp.bfloat16)
```

```python
import jax
import jax.numpy as jnp
from jax import lax
from jax.sharding import PartitionSpec as P

BLOCK = 256


def passed_along(value, axis, by):
    count = lax.axis_size(axis)
    pairs = [(i, i + by) for i in range(count) if 0 <= i + by < count]
    return lax.ppermute(value, axis, pairs)


def convolve(values, edge_rows, weights, in_block, carry_on):
    lag_rows = weights.shape[0] - 1
    row_total = values.shape[0]
    widened = jnp.concatenate([edge_rows, values], axis=0).astype(jnp.float32)
    total = jnp.zeros(values.shape, jnp.float32)
    for offset in range(weights.shape[0]):
        shifted = widened[lag_rows - offset : lag_rows - offset + row_total]
        keeping = (in_block >= offset) | carry_on
        total = total + jnp.where(keeping[:, None], shifted, 0.0) * weights[offset]
    return jax.nn.silu(total).astype(jnp.bfloat16)


def on_device(
    tokens,
    w_inner,
    w_states,
    w_step,
    conv_inner,
    conv_states,
    decay_rate,
    step_bias,
    skip_gain,
    norm_gain,
    w_output,
    block_owner,
    lengths,
):
    row_count = tokens.shape[0]
    local_blocks = row_count // BLOCK
    total_blocks = block_owner.shape[0]
    heads_here = w_step.shape[1]
    inner_here = w_inner.shape[2]
    state_size = w_states.shape[1] // 2
    head_size = inner_here // heads_here
    lag_rows = conv_inner.shape[0] - 1
    block_ids = jnp.arange(total_blocks, dtype=jnp.int32)
    same_owner = block_owner[:, None] == block_owner[None, :]
    first_block = jnp.min(jnp.where(same_owner, block_ids[None, :], total_blocks), axis=1)
    starting = (first_block == block_ids).astype(jnp.int32)
    request_ids = jnp.arange(lengths.shape[0], dtype=jnp.int32)
    own_length = jnp.sum(
        jnp.where(block_owner[:, None] == request_ids[None, :], lengths[None, :], 0), axis=1
    )
    valid_rows = jnp.clip(own_length - (block_ids - first_block) * BLOCK, 0, BLOCK)
    seq_index = lax.axis_index("seq")
    local_start = lax.dynamic_slice_in_dim(starting, seq_index * local_blocks, local_blocks)
    local_valid = lax.dynamic_slice_in_dim(valid_rows, seq_index * local_blocks, local_blocks)
    in_block = jnp.arange(row_count, dtype=jnp.int32) % BLOCK
    carry_on = jnp.repeat(local_start == 0, BLOCK)
    whole = lax.all_gather(tokens, "tp", axis=1, tiled=True)
    pieces = (
        lax.all_gather(w_inner, "seq", axis=0, tiled=True),
        lax.all_gather(w_states, "seq", axis=0, tiled=True),
        lax.all_gather(w_step, "seq", axis=0, tiled=True),
    )
    count = pieces[0].shape[0]
    inner_sum = jnp.dot(
        whole, pieces[0].reshape(count, 2 * inner_here), preferred_element_type=jnp.float32
    )
    states_sum = jnp.dot(whole, pieces[1], preferred_element_type=jnp.float32)
    step_sum = jnp.dot(whole, pieces[2], preferred_element_type=jnp.float32)
    projected = inner_sum.astype(jnp.bfloat16)
    gate_in = projected[:, :inner_here]
    x_in = projected[:, inner_here:]
    bc_in = states_sum.astype(jnp.bfloat16)
    step_raw = step_sum.astype(jnp.bfloat16)
    edge_inner, edge_states = passed_along(
        (x_in[row_count - lag_rows :], bc_in[row_count - lag_rows :]), "seq", 1
    )
    x_conv = convolve(x_in, edge_inner, conv_inner, in_block, carry_on)
    bc_conv = convolve(bc_in, edge_states, conv_states, in_block, carry_on)
    step_size = jax.nn.softplus(step_raw.astype(jnp.float32) + step_bias)
    log_decay = -decay_rate * step_size
    x_heads = x_conv.reshape(local_blocks, BLOCK, heads_here, head_size)
    b_rows = bc_conv[:, :state_size].reshape(local_blocks, BLOCK, state_size)
    c_rows = bc_conv[:, state_size:].reshape(local_blocks, BLOCK, state_size)
    step_blocks = step_size.reshape(local_blocks, BLOCK, heads_here)
    cumulative = jnp.cumsum(log_decay.reshape(local_blocks, BLOCK, heads_here), axis=1)
    causal = jnp.arange(BLOCK)[:, None] >= jnp.arange(BLOCK)[None, :]
    spread = cumulative[:, :, None, :] - cumulative[:, None, :, :]
    decays = jnp.exp(jnp.where(causal[None, :, :, None], spread, -jnp.inf))
    intersection = jnp.einsum("cin,cjn->cij", c_rows, b_rows, preferred_element_type=jnp.float32)
    mixing = (decays * intersection[:, :, :, None] * step_blocks[:, None, :, :]).astype(
        jnp.bfloat16
    )
    y_inner = jnp.einsum("cijh,cjhp->cihp", mixing, x_heads, preferred_element_type=jnp.float32)
    final_log = cumulative[:, -1, :]
    tail_weight = jnp.exp(final_log[:, None, :] - cumulative) * step_blocks
    weighted_b = (tail_weight[:, :, :, None] * b_rows.astype(jnp.float32)[:, :, None, :]).astype(
        jnp.bfloat16
    )
    fresh = jnp.einsum("cjhn,cjhp->chnp", weighted_b, x_heads, preferred_element_type=jnp.float32)
    keep_flag = jnp.where(local_start == 1, 0.0, 1.0).astype(jnp.float32)
    block_gain_each = jnp.exp(final_log) * keep_flag[:, None]

    def fold_block(carry, item):
        gain_now, fresh_now = item
        return ((carry[0] * gain_now, gain_now[:, None, None] * carry[1] + fresh_now), None)

    zero_state = jnp.zeros((heads_here, state_size, head_size), jnp.float32)
    unit_gain = jnp.ones((heads_here,), jnp.float32)
    (block_gain, block_state), _ = lax.scan(
        fold_block, (unit_gain, zero_state), (block_gain_each, fresh)
    )

    seq_count = lax.axis_size("seq")
    reach = min(seq_count - 1, -(-(total_blocks // 2) // local_blocks))
    gains = lax.all_gather(block_gain, "seq", axis=0)
    sent_state = block_state.astype(jnp.bfloat16)
    entering = zero_state
    factor = unit_gain
    for distance in range(1, reach + 1):
        arrived = passed_along(sent_state, "seq", distance)
        entering = entering + factor[:, None, None] * arrived.astype(jnp.float32)
        source = jnp.maximum(seq_index - distance, 0)
        factor = factor * lax.dynamic_index_in_dim(gains, source, 0, keepdims=False)

    def pass_block(previous, item):
        log_now, keep_now, fresh_now = item
        incoming = previous * keep_now
        return (jnp.exp(log_now)[:, None, None] * incoming + fresh_now, incoming)

    _, incoming_all = lax.scan(pass_block, entering, (final_log, keep_flag, fresh))
    incoming_half = incoming_all.astype(jnp.bfloat16)
    y_carry = jnp.exp(cumulative)[:, :, :, None] * jnp.einsum(
        "cin,chnp->cihp", c_rows, incoming_half, preferred_element_type=jnp.float32
    )
    y_total = (y_inner + y_carry).reshape(row_count, inner_here) + jnp.repeat(skip_gain, head_size)[
        None, :
    ] * x_conv.astype(jnp.float32)
    gated = y_total * jax.nn.silu(gate_in.astype(jnp.float32))
    squares = lax.psum(jnp.sum(gated * gated, axis=1), "tp")
    square_mean = squares / (inner_here * lax.axis_size("tp"))
    normed = (gated * norm_gain).astype(jnp.bfloat16)
    partial_out = jnp.dot(
        normed,
        lax.all_gather(w_output, "seq", axis=1, tiled=True),
        preferred_element_type=jnp.float32,
    )
    summed = lax.psum_scatter(
        partial_out.astype(jnp.bfloat16), "tp", scatter_dimension=1, tiled=True
    ).astype(jnp.float32) * lax.rsqrt(square_mean + 1e-05)[:, None]
    live = in_block < jnp.repeat(local_valid, BLOCK)
    return jnp.where(live[:, None], summed, 0.0).astype(jnp.bfloat16)


def solution(mesh):
    return jax.shard_map(
        on_device,
        mesh=mesh,
        in_specs=(
            P("seq", "tp"),
            P("seq", None, "tp"),
            P("seq", None),
            P("seq", "tp"),
            P(None, "tp"),
            P(),
            P("tp"),
            P("tp"),
            P("tp"),
            P("tp"),
            P("tp", "seq"),
            P(),
            P(),
        ),
        out_specs=P("seq", "tp"),
        check_vma=False,
    )
```

```python
import functools

import jax
import jax.numpy as jnp
from jax import lax
from jax.experimental import pallas as pl
from jax.experimental.pallas import tpu as pltpu
from jax.sharding import PartitionSpec as P

BLOCK = 256


def passed_along(value, axis, by):
    count = lax.axis_size(axis)
    pairs = [(i, i + by) for i in range(count) if 0 <= i + by < count]
    return lax.ppermute(value, axis, pairs)


def convolve(values, edge_rows, weights, in_block, carry_on):
    lag_rows = weights.shape[0] - 1
    row_total = values.shape[0]
    widened = jnp.concatenate([edge_rows, values], axis=0).astype(jnp.float32)
    total = jnp.zeros(values.shape, jnp.float32)
    for offset in range(weights.shape[0]):
        shifted = widened[lag_rows - offset : lag_rows - offset + row_total]
        keeping = (in_block >= offset) | carry_on
        total = total + jnp.where(keeping[:, None], shifted, 0.0) * weights[offset]
    return jax.nn.silu(total).astype(jnp.bfloat16)


LANES = 128
ROW_CHUNK = 256
VMEM_BYTES = 50 * 1024 * 1024


def spread_heads(columns, tile, head_size):
    per_tile = LANES // head_size
    lane = lax.broadcasted_iota(jnp.int32, (columns.shape[0], LANES), 1)
    result = columns[:, tile * per_tile : tile * per_tile + 1]
    for k in range(1, per_tile):
        head = tile * per_tile + k
        result = jnp.where(lane < k * head_size, result, columns[:, head : head + 1])
    return result


def state_kernel(head_size, x_ref, bc_ref, cum_ref, step_ref, gain_ref, fresh_ref, total_ref):
    block = pl.program_id(0)
    state_size = bc_ref.shape[1] // 2

    @pl.when(block == 0)
    def _():
        total_ref[...] = jnp.zeros_like(total_ref)

    cum = cum_ref[...]
    tail = jnp.exp(cum[BLOCK - 1 : BLOCK, :] - cum) * step_ref[...]
    b_rows = bc_ref[:, :state_size]
    for tile in range(x_ref.shape[1] // LANES):
        cols = slice(tile * LANES, (tile + 1) * LANES)
        weighted = x_ref[:, cols].astype(jnp.float32) * spread_heads(tail, tile, head_size)
        fresh = lax.dot_general(
            b_rows,
            weighted.astype(jnp.bfloat16),
            (((0,), (0,)), ((), ())),
            preferred_element_type=jnp.float32,
        )
        fresh_ref[0, :, cols] = fresh
        total_ref[:, cols] = total_ref[:, cols] * gain_ref[0, :, cols] + fresh


def mix_kernel(
    head_size,
    x_ref,
    bc_ref,
    gate_ref,
    cum_ref,
    cum_t_ref,
    step_t_ref,
    gain_ref,
    keep_ref,
    fresh_ref,
    entering_ref,
    skip_ref,
    norm_ref,
    out_ref,
    square_ref,
    state_ref,
):
    block = pl.program_id(0)
    state_size = bc_ref.shape[1] // 2
    per_tile = LANES // head_size

    @pl.when(block == 0)
    def _():
        state_ref[...] = entering_ref[...]

    b_rows = bc_ref[:, :state_size]
    c_rows = bc_ref[:, state_size:]
    products = lax.dot_general(
        c_rows, b_rows, (((1,), (1,)), ((), ())), preferred_element_type=jnp.float32
    )
    rows = lax.broadcasted_iota(jnp.int32, (BLOCK, BLOCK), 0)
    causal = rows >= lax.broadcasted_iota(jnp.int32, (BLOCK, BLOCK), 1)
    lane = lax.broadcasted_iota(jnp.int32, (BLOCK, LANES), 1)
    cum = cum_ref[...]
    grown = jnp.exp(cum)
    squares = jnp.zeros((BLOCK, LANES), jnp.float32)
    for tile in range(x_ref.shape[1] // LANES):
        cols = slice(tile * LANES, (tile + 1) * LANES)
        x_tile = x_ref[:, cols]
        y_tile = None
        for k in range(per_tile):
            head = tile * per_tile + k
            spread = cum[:, head : head + 1] - cum_t_ref[head : head + 1, :]
            decays = jnp.exp(jnp.where(causal, spread, -jnp.inf))
            mixing = decays * products * step_t_ref[head : head + 1, :]
            part = jnp.dot(
                mixing.astype(jnp.bfloat16), x_tile, preferred_element_type=jnp.float32
            )
            y_tile = part if k == 0 else jnp.where(lane < k * head_size, y_tile, part)
        previous = state_ref[:, cols]
        incoming = (previous * keep_ref[0, :, cols]).astype(jnp.bfloat16)
        carried = jnp.dot(c_rows, incoming, preferred_element_type=jnp.float32)
        state_ref[:, cols] = previous * gain_ref[0, :, cols] + fresh_ref[0, :, cols]
        y_tile = y_tile + spread_heads(grown, tile, head_size) * carried
        y_tile = y_tile + skip_ref[:, cols] * x_tile.astype(jnp.float32)
        gate = gate_ref[:, cols].astype(jnp.float32)
        gated = y_tile * (gate * jax.nn.sigmoid(gate))
        squares = squares + gated * gated
        out_ref[:, cols] = (gated * norm_ref[:, cols]).astype(jnp.bfloat16)
    square_ref[...] = jnp.sum(squares, axis=1, keepdims=True)


def output_kernel(
    tp_count, a_ref, w_ref, out_ref, send_a, recv_a, send_b, recv_b, sa_sem, ra_sem, sb_sem, rb_sem
):
    mesh_id = pl.DeviceIdType.MESH
    chips = tp_count // 2
    width = out_ref.shape[1]
    chunks = out_ref.shape[0] // ROW_CHUNK
    me = lax.axis_index("tp")
    chip = me // 2
    core = lax.rem(me, 2)
    partner = chip * 2 + (1 - core)

    def chip_at(offset):
        return lax.rem(chip + offset, chips)

    barrier = pltpu.get_barrier_semaphore()
    pl.semaphore_signal(barrier, inc=1, device_id={"tp": partner}, device_id_type=mesh_id)
    for offset in range(1, chips):
        pl.semaphore_signal(
            barrier,
            inc=1,
            device_id={"tp": chip_at(offset) * 2 + core},
            device_id_type=mesh_id,
        )
    pl.semaphore_wait(barrier, chips)

    def product(chunk, owner):
        columns = pl.ds(pl.multiple_of(owner * width, LANES), width)
        return jnp.dot(
            a_ref[chunk * ROW_CHUNK : (chunk + 1) * ROW_CHUNK, :],
            w_ref[:, columns],
            preferred_element_type=jnp.float32,
        )

    def to_partner(chunk, offset):
        return pltpu.make_async_remote_copy(
            src_ref=send_a.at[chunk, offset],
            dst_ref=recv_a.at[chunk, offset],
            send_sem=sa_sem.at[chunk, offset],
            recv_sem=ra_sem.at[chunk, offset],
            device_id={"tp": partner},
            device_id_type=mesh_id,
        )

    def to_chip(chunk, offset):
        return pltpu.make_async_remote_copy(
            src_ref=send_b.at[chunk, offset - 1],
            dst_ref=recv_b.at[chunk, offset - 1],
            send_sem=sb_sem.at[chunk, offset - 1],
            recv_sem=rb_sem.at[chunk, offset - 1],
            device_id={"tp": chip_at(offset) * 2 + core},
            device_id_type=mesh_id,
        )

    def first_half(chunk, offset):
        send_a[chunk, offset] = product(chunk, chip_at(offset) * 2 + 1 - core).astype(jnp.bfloat16)
        to_partner(chunk, offset).start()

    def second_half(chunk, offset):
        own = product(chunk, chip_at(offset) * 2 + core)
        to_partner(chunk, offset).wait()
        send_b[chunk, offset - 1] = (own + recv_a[chunk, offset].astype(jnp.float32)).astype(
            jnp.bfloat16
        )
        to_chip(chunk, offset).start()

    for chunk in range(chunks):
        for offset in range(1, chips):
            first_half(chunk, offset)
            if chunk > 0:
                second_half(chunk - 1, offset)
    for offset in range(1, chips):
        second_half(chunks - 1, offset)
    for chunk in range(chunks):
        first_half(chunk, 0)
    for chunk in range(chunks):
        own = product(chunk, me)
        to_partner(chunk, 0).wait()
        total = own + recv_a[chunk, 0].astype(jnp.float32)
        for offset in range(1, chips):
            to_chip(chunk, offset).wait()
            total = total + recv_b[chunk, offset - 1].astype(jnp.float32)
        out_ref[chunk * ROW_CHUNK : (chunk + 1) * ROW_CHUNK, :] = total


def projected_sum(rows, weights, tp_count):
    row_count, width = rows.shape[0], weights.shape[1] // tp_count
    chunks, chips = row_count // ROW_CHUNK, tp_count // 2
    vmem = pl.BlockSpec(memory_space=pltpu.VMEM)
    return pl.pallas_call(
        functools.partial(output_kernel, tp_count),
        out_shape=jax.ShapeDtypeStruct((row_count, width), jnp.float32),
        in_specs=[vmem, vmem],
        out_specs=vmem,
        scratch_shapes=[
            pltpu.VMEM((chunks, chips, ROW_CHUNK, width), jnp.bfloat16),
            pltpu.VMEM((chunks, chips, ROW_CHUNK, width), jnp.bfloat16),
            pltpu.VMEM((chunks, chips - 1, ROW_CHUNK, width), jnp.bfloat16),
            pltpu.VMEM((chunks, chips - 1, ROW_CHUNK, width), jnp.bfloat16),
            pltpu.SemaphoreType.DMA((chunks, chips)),
            pltpu.SemaphoreType.DMA((chunks, chips)),
            pltpu.SemaphoreType.DMA((chunks, chips - 1)),
            pltpu.SemaphoreType.DMA((chunks, chips - 1)),
        ],
        compiler_params=pltpu.CompilerParams(
            collective_id=3, has_side_effects=True, vmem_limit_bytes=VMEM_BYTES
        ),
        name="output_kernel",
    )(rows, weights)


def on_device(
    tokens,
    w_inner,
    w_states,
    w_step,
    conv_inner,
    conv_states,
    decay_rate,
    step_bias,
    skip_gain,
    norm_gain,
    w_output,
    block_owner,
    lengths,
):
    row_count = tokens.shape[0]
    local_blocks = row_count // BLOCK
    total_blocks = block_owner.shape[0]
    heads_here = w_step.shape[1]
    inner_here = w_inner.shape[2]
    state_size = w_states.shape[1] // 2
    head_size = inner_here // heads_here
    lag_rows = conv_inner.shape[0] - 1
    block_ids = jnp.arange(total_blocks, dtype=jnp.int32)
    same_owner = block_owner[:, None] == block_owner[None, :]
    first_block = jnp.min(jnp.where(same_owner, block_ids[None, :], total_blocks), axis=1)
    starting = (first_block == block_ids).astype(jnp.int32)
    request_ids = jnp.arange(lengths.shape[0], dtype=jnp.int32)
    own_length = jnp.sum(
        jnp.where(block_owner[:, None] == request_ids[None, :], lengths[None, :], 0), axis=1
    )
    valid_rows = jnp.clip(own_length - (block_ids - first_block) * BLOCK, 0, BLOCK)
    seq_index = lax.axis_index("seq")
    local_start = lax.dynamic_slice_in_dim(starting, seq_index * local_blocks, local_blocks)
    local_valid = lax.dynamic_slice_in_dim(valid_rows, seq_index * local_blocks, local_blocks)
    in_block = jnp.arange(row_count, dtype=jnp.int32) % BLOCK
    carry_on = jnp.repeat(local_start == 0, BLOCK)
    whole = lax.all_gather(tokens, "tp", axis=1, tiled=True)
    shard = jnp.concatenate(
        [w_inner.reshape(w_inner.shape[0], 2 * inner_here), w_states, w_step], axis=1
    )
    weights = lax.all_gather(shard, "seq", axis=0, tiled=True)
    projected = jnp.dot(whole, weights, preferred_element_type=jnp.float32).astype(jnp.bfloat16)
    states_end = 2 * inner_here + 2 * state_size
    x_in = projected[:, inner_here : 2 * inner_here]
    bc_in = projected[:, 2 * inner_here : states_end]
    step_raw = projected[:, states_end:]
    edges = passed_along(projected[row_count - lag_rows :, inner_here:states_end], "seq", 1)
    edge_inner, edge_states = edges[:, :inner_here], edges[:, inner_here:]
    x_conv = convolve(x_in, edge_inner, conv_inner, in_block, carry_on)
    bc_conv = convolve(bc_in, edge_states, conv_states, in_block, carry_on)
    step_size = jax.nn.softplus(step_raw.astype(jnp.float32) + step_bias)
    log_decay = -decay_rate * step_size
    cumulative = jnp.cumsum(log_decay.reshape(local_blocks, BLOCK, heads_here), axis=1)
    final_log = cumulative[:, -1, :]
    keep_flag = jnp.where(local_start == 1, 0.0, 1.0).astype(jnp.float32)
    block_gain_each = jnp.exp(final_log) * keep_flag[:, None]
    gain_lanes = jnp.repeat(block_gain_each, head_size, axis=1)[:, None, :]
    keep_lanes = jnp.broadcast_to(keep_flag[:, None, None], gain_lanes.shape)
    cum_rows = cumulative.reshape(row_count, heads_here)
    by_rows = lambda width: pl.BlockSpec((BLOCK, width), lambda c: (c, 0))
    by_block = lambda *dims: pl.BlockSpec((1,) + dims, lambda c: (c, 0, 0))
    fixed = lambda *dims: pl.BlockSpec(dims, lambda c: (0, 0))
    turned = pl.BlockSpec((heads_here, BLOCK), lambda c: (0, c))
    params = pltpu.CompilerParams(vmem_limit_bytes=VMEM_BYTES)
    fresh, block_state = pl.pallas_call(
        functools.partial(state_kernel, head_size),
        grid=(local_blocks,),
        in_specs=[
            by_rows(inner_here),
            by_rows(2 * state_size),
            by_rows(heads_here),
            by_rows(heads_here),
            by_block(1, inner_here),
        ],
        out_specs=[by_block(state_size, inner_here), fixed(state_size, inner_here)],
        out_shape=[
            jax.ShapeDtypeStruct((local_blocks, state_size, inner_here), jnp.float32),
            jax.ShapeDtypeStruct((state_size, inner_here), jnp.float32),
        ],
        compiler_params=params,
        name="state_kernel",
    )(x_conv, bc_conv, cum_rows, step_size, gain_lanes)
    seq_count = lax.axis_size("seq")
    reach = min(seq_count - 1, -(-(total_blocks // 2) // local_blocks))
    device_gain = jnp.prod(gain_lanes, axis=0)
    gain_high = device_gain.astype(jnp.bfloat16)
    gain_low = (device_gain - gain_high.astype(jnp.float32)).astype(jnp.bfloat16)
    message = jnp.concatenate(
        [
            block_state.astype(jnp.bfloat16),
            jnp.broadcast_to(gain_high, (8, inner_here)),
            jnp.broadcast_to(gain_low, (8, inner_here)),
        ],
        axis=0,
    )
    entering = jnp.zeros((state_size, inner_here), jnp.float32)
    factor = jnp.ones((1, inner_here), jnp.float32)
    for distance in range(1, reach + 1):
        arrived = passed_along(message, "seq", distance).astype(jnp.float32)
        entering = entering + factor * arrived[:state_size]
        factor = factor * (
            arrived[state_size : state_size + 1] + arrived[state_size + 8 : state_size + 9]
        )
    normed, squares_here = pl.pallas_call(
        functools.partial(mix_kernel, head_size),
        grid=(local_blocks,),
        in_specs=[
            by_rows(inner_here),
            by_rows(2 * state_size),
            by_rows(inner_here),
            by_rows(heads_here),
            turned,
            turned,
            by_block(1, inner_here),
            by_block(1, inner_here),
            by_block(state_size, inner_here),
            fixed(state_size, inner_here),
            fixed(1, inner_here),
            fixed(1, inner_here),
        ],
        out_specs=[by_rows(inner_here), by_rows(1)],
        out_shape=[
            jax.ShapeDtypeStruct((row_count, inner_here), jnp.bfloat16),
            jax.ShapeDtypeStruct((row_count, 1), jnp.float32),
        ],
        scratch_shapes=[pltpu.VMEM((state_size, inner_here), jnp.float32)],
        compiler_params=params,
        name="mix_kernel",
    )(
        x_conv,
        bc_conv,
        projected,
        cum_rows,
        cum_rows.T,
        step_size.T,
        gain_lanes,
        keep_lanes,
        fresh,
        entering,
        jnp.repeat(skip_gain, head_size)[None, :],
        norm_gain[None, :],
    )
    tp_count = lax.axis_size("tp")
    squares = lax.psum(squares_here[:, 0], "tp")
    square_mean = squares / (inner_here * tp_count)
    summed = projected_sum(normed, lax.all_gather(w_output, "seq", axis=1, tiled=True), tp_count)
    summed = summed * lax.rsqrt(square_mean + 1e-05)[:, None]
    live = in_block < jnp.repeat(local_valid, BLOCK)
    return jnp.where(live[:, None], summed, 0.0).astype(jnp.bfloat16)


def solution(mesh):
    return jax.shard_map(
        on_device,
        mesh=mesh,
        in_specs=(
            P("seq", "tp"),
            P("seq", None, "tp"),
            P("seq", None),
            P("seq", "tp"),
            P(None, "tp"),
            P(),
            P("tp"),
            P("tp"),
            P("tp"),
            P("tp"),
            P("tp", "seq"),
            P(),
            P(),
        ),
        out_specs=P("seq", "tp"),
        check_vma=False,
    )
```

```python
import functools

import jax
import jax.numpy as jnp
from jax import lax
from jax.experimental import pallas as pl
from jax.experimental.pallas import tpu as pltpu
from jax.sharding import PartitionSpec as P

BLOCK = 256


def passed_along(value, axis, by):
    count = lax.axis_size(axis)
    pairs = [(i, i + by) for i in range(count) if 0 <= i + by < count]
    return lax.ppermute(value, axis, pairs)


def convolve(values, edge_rows, weights, in_block, carry_on):
    lag_rows = weights.shape[0] - 1
    row_total = values.shape[0]
    widened = jnp.concatenate([edge_rows, values], axis=0).astype(jnp.float32)
    total = jnp.zeros(values.shape, jnp.float32)
    for offset in range(weights.shape[0]):
        shifted = widened[lag_rows - offset : lag_rows - offset + row_total]
        keeping = (in_block >= offset) | carry_on
        total = total + jnp.where(keeping[:, None], shifted, 0.0) * weights[offset]
    return jax.nn.silu(total).astype(jnp.bfloat16)


LANES = 128
ROW_CHUNK = 256
VMEM_BYTES = 50 * 1024 * 1024


def spread_heads(columns, tile, head_size):
    per_tile = LANES // head_size
    lane = lax.broadcasted_iota(jnp.int32, (columns.shape[0], LANES), 1)
    result = columns[:, tile * per_tile : tile * per_tile + 1]
    for k in range(1, per_tile):
        head = tile * per_tile + k
        result = jnp.where(lane < k * head_size, result, columns[:, head : head + 1])
    return result


def state_kernel(head_size, x_ref, bc_ref, cum_ref, step_ref, gain_ref, fresh_ref, total_ref):
    block = pl.program_id(0)
    state_size = bc_ref.shape[1] // 2

    @pl.when(block == 0)
    def _():
        total_ref[...] = jnp.zeros_like(total_ref)

    cum = cum_ref[...]
    tail = jnp.exp(cum[BLOCK - 1 : BLOCK, :] - cum) * step_ref[...]
    b_rows = bc_ref[:, :state_size]
    for tile in range(x_ref.shape[1] // LANES):
        cols = slice(tile * LANES, (tile + 1) * LANES)
        weighted = x_ref[:, cols].astype(jnp.float32) * spread_heads(tail, tile, head_size)
        fresh = lax.dot_general(
            b_rows,
            weighted.astype(jnp.bfloat16),
            (((0,), (0,)), ((), ())),
            preferred_element_type=jnp.float32,
        )
        fresh_ref[0, :, cols] = fresh
        total_ref[:, cols] = total_ref[:, cols] * gain_ref[0, :, cols] + fresh


def mix_kernel(
    head_size,
    x_ref,
    bc_ref,
    gate_ref,
    cum_ref,
    cum_t_ref,
    step_t_ref,
    gain_ref,
    keep_ref,
    fresh_ref,
    entering_ref,
    skip_ref,
    norm_ref,
    out_ref,
    square_ref,
    state_ref,
):
    block = pl.program_id(0)
    state_size = bc_ref.shape[1] // 2
    per_tile = LANES // head_size

    @pl.when(block == 0)
    def _():
        state_ref[...] = entering_ref[...]

    b_rows = bc_ref[:, :state_size]
    c_rows = bc_ref[:, state_size:]
    products = lax.dot_general(
        c_rows, b_rows, (((1,), (1,)), ((), ())), preferred_element_type=jnp.float32
    )
    rows = lax.broadcasted_iota(jnp.int32, (BLOCK, BLOCK), 0)
    causal = rows >= lax.broadcasted_iota(jnp.int32, (BLOCK, BLOCK), 1)
    lane = lax.broadcasted_iota(jnp.int32, (BLOCK, LANES), 1)
    cum = cum_ref[...]
    grown = jnp.exp(cum)
    squares = jnp.zeros((BLOCK, LANES), jnp.float32)
    for tile in range(x_ref.shape[1] // LANES):
        cols = slice(tile * LANES, (tile + 1) * LANES)
        x_tile = x_ref[:, cols]
        y_tile = None
        for k in range(per_tile):
            head = tile * per_tile + k
            spread = cum[:, head : head + 1] - cum_t_ref[head : head + 1, :]
            decays = jnp.exp(jnp.where(causal, spread, -jnp.inf))
            mixing = decays * products * step_t_ref[head : head + 1, :]
            part = jnp.dot(
                mixing.astype(jnp.bfloat16), x_tile, preferred_element_type=jnp.float32
            )
            y_tile = part if k == 0 else jnp.where(lane < k * head_size, y_tile, part)
        previous = state_ref[:, cols]
        incoming = (previous * keep_ref[0, :, cols]).astype(jnp.bfloat16)
        carried = jnp.dot(c_rows, incoming, preferred_element_type=jnp.float32)
        state_ref[:, cols] = previous * gain_ref[0, :, cols] + fresh_ref[0, :, cols]
        y_tile = y_tile + spread_heads(grown, tile, head_size) * carried
        y_tile = y_tile + skip_ref[:, cols] * x_tile.astype(jnp.float32)
        gate = gate_ref[:, cols].astype(jnp.float32)
        gated = y_tile * (gate * jax.nn.sigmoid(gate))
        squares = squares + gated * gated
        out_ref[:, cols] = (gated * norm_ref[:, cols]).astype(jnp.bfloat16)
    square_ref[...] = jnp.sum(squares, axis=1, keepdims=True)


def output_kernel(
    tp_count, a_ref, w_ref, out_ref, send_a, recv_a, send_b, recv_b, sa_sem, ra_sem, sb_sem, rb_sem
):
    mesh_id = pl.DeviceIdType.MESH
    chips = tp_count // 2
    width = out_ref.shape[1]
    chunks = out_ref.shape[0] // ROW_CHUNK
    me = lax.axis_index("tp")
    chip = me // 2
    core = lax.rem(me, 2)
    partner = chip * 2 + (1 - core)

    def chip_at(offset):
        return lax.rem(chip + offset, chips)

    barrier = pltpu.get_barrier_semaphore()
    pl.semaphore_signal(barrier, inc=1, device_id={"tp": partner}, device_id_type=mesh_id)
    for offset in range(1, chips):
        pl.semaphore_signal(
            barrier,
            inc=1,
            device_id={"tp": chip_at(offset) * 2 + core},
            device_id_type=mesh_id,
        )
    pl.semaphore_wait(barrier, chips)

    def product(chunk, owner):
        columns = pl.ds(pl.multiple_of(owner * width, LANES), width)
        return jnp.dot(
            a_ref[chunk * ROW_CHUNK : (chunk + 1) * ROW_CHUNK, :],
            w_ref[:, columns],
            preferred_element_type=jnp.float32,
        )

    def to_partner(chunk, offset):
        return pltpu.make_async_remote_copy(
            src_ref=send_a.at[chunk, offset],
            dst_ref=recv_a.at[chunk, offset],
            send_sem=sa_sem.at[chunk, offset],
            recv_sem=ra_sem.at[chunk, offset],
            device_id={"tp": partner},
            device_id_type=mesh_id,
        )

    def to_chip(chunk, offset):
        return pltpu.make_async_remote_copy(
            src_ref=send_b.at[chunk, offset - 1],
            dst_ref=recv_b.at[chunk, offset - 1],
            send_sem=sb_sem.at[chunk, offset - 1],
            recv_sem=rb_sem.at[chunk, offset - 1],
            device_id={"tp": chip_at(offset) * 2 + core},
            device_id_type=mesh_id,
        )

    def first_half(chunk, offset):
        send_a[chunk, offset] = product(chunk, chip_at(offset) * 2 + 1 - core).astype(jnp.bfloat16)
        to_partner(chunk, offset).start()

    def second_half(chunk, offset):
        own = product(chunk, chip_at(offset) * 2 + core)
        to_partner(chunk, offset).wait()
        send_b[chunk, offset - 1] = (own + recv_a[chunk, offset].astype(jnp.float32)).astype(
            jnp.bfloat16
        )
        to_chip(chunk, offset).start()

    for chunk in range(chunks):
        for offset in range(1, chips):
            first_half(chunk, offset)
            if chunk > 0:
                second_half(chunk - 1, offset)
    for offset in range(1, chips):
        second_half(chunks - 1, offset)
    for chunk in range(chunks):
        first_half(chunk, 0)
    for chunk in range(chunks):
        own = product(chunk, me)
        to_partner(chunk, 0).wait()
        total = own + recv_a[chunk, 0].astype(jnp.float32)
        for offset in range(1, chips):
            to_chip(chunk, offset).wait()
            total = total + recv_b[chunk, offset - 1].astype(jnp.float32)
        out_ref[chunk * ROW_CHUNK : (chunk + 1) * ROW_CHUNK, :] = total


def projected_sum(rows, weights, tp_count):
    row_count, width = rows.shape[0], weights.shape[1] // tp_count
    chunks, chips = row_count // ROW_CHUNK, tp_count // 2
    vmem = pl.BlockSpec(memory_space=pltpu.VMEM)
    return pl.pallas_call(
        functools.partial(output_kernel, tp_count),
        out_shape=jax.ShapeDtypeStruct((row_count, width), jnp.float32),
        in_specs=[vmem, vmem],
        out_specs=vmem,
        scratch_shapes=[
            pltpu.VMEM((chunks, chips, ROW_CHUNK, width), jnp.bfloat16),
            pltpu.VMEM((chunks, chips, ROW_CHUNK, width), jnp.bfloat16),
            pltpu.VMEM((chunks, chips - 1, ROW_CHUNK, width), jnp.bfloat16),
            pltpu.VMEM((chunks, chips - 1, ROW_CHUNK, width), jnp.bfloat16),
            pltpu.SemaphoreType.DMA((chunks, chips)),
            pltpu.SemaphoreType.DMA((chunks, chips)),
            pltpu.SemaphoreType.DMA((chunks, chips - 1)),
            pltpu.SemaphoreType.DMA((chunks, chips - 1)),
        ],
        compiler_params=pltpu.CompilerParams(
            collective_id=3, has_side_effects=True, vmem_limit_bytes=VMEM_BYTES
        ),
        name="output_kernel",
    )(rows, weights)


def gather_kernel(
    seq_count, tp_count, rows_ref, shard_ref, whole_ref, slots_ref, own_sem, line_sem, fan_sem,
    slot_sem, peer_send, peer_recv
):
    mesh_id = pl.DeviceIdType.MESH
    slow = 4 if seq_count % 4 == 0 else 1
    fast = seq_count // slow
    me = lax.axis_index("seq")
    a, b = me // fast, lax.rem(me, fast)
    t = lax.axis_index("tp")
    width = rows_ref.shape[1]
    barrier = pltpu.get_barrier_semaphore()

    def greet(device):
        pl.semaphore_signal(barrier, inc=1, device_id=device, device_id_type=mesh_id)

    @pl.when(a > 0)
    def _():
        greet({"seq": me - fast})

    @pl.when(a < slow - 1)
    def _():
        greet({"seq": me + fast})

    for k in range(1, fast):
        greet({"seq": a * fast + lax.rem(b + k, fast)})
    for k in range(1, tp_count):
        greet({"tp": lax.rem(t + k, tp_count)})

    inside = (a > 0).astype(jnp.int32) + (a < slow - 1).astype(jnp.int32)
    pl.semaphore_wait(barrier, inside + (fast - 1 + tp_count - 1))

    def shard_copy(source, origin_a, origin_b, send_sem, target):
        return pltpu.make_async_remote_copy(
            src_ref=source,
            dst_ref=slots_ref.at[origin_a * fast + origin_b],
            send_sem=send_sem,
            recv_sem=slot_sem.at[origin_a * fast + origin_b],
            device_id={"seq": target},
            device_id_type=mesh_id,
        )

    def to_right(source, origin):
        return shard_copy(source, origin, b, line_sem.at[0, origin], me + fast)

    def to_left(source, origin):
        return shard_copy(source, origin, b, line_sem.at[1, origin], me - fast)

    def to_fan(source, origin, k):
        target = a * fast + lax.rem(b + k, fast)
        return shard_copy(source, origin, b, fan_sem.at[origin, k - 1], target)

    def peer_copy(k):
        return pltpu.make_async_remote_copy(
            src_ref=rows_ref,
            dst_ref=whole_ref.at[:, pl.ds(pl.multiple_of(t * width, LANES), width)],
            send_sem=peer_send.at[k - 1],
            recv_sem=peer_recv.at[k - 1],
            device_id={"tp": lax.rem(t + k, tp_count)},
            device_id_type=mesh_id,
        )

    @pl.when(a < slow - 1)
    def _():
        to_right(shard_ref, a).start()

    @pl.when(a > 0)
    def _():
        to_left(shard_ref, a).start()

    for k in range(1, fast):
        to_fan(shard_ref, a, k).start()
    for k in range(1, tp_count):
        peer_copy(k).start()
    own_shard = pltpu.make_async_copy(shard_ref, slots_ref.at[me], own_sem.at[0])
    own_rows = pltpu.make_async_copy(
        rows_ref,
        whole_ref.at[:, pl.ds(pl.multiple_of(t * width, LANES), width)],
        own_sem.at[1],
    )
    own_shard.start()
    own_rows.start()

    for step in range(1, slow):

        @pl.when(a - step >= 0)
        def _():
            origin = a - step
            source = slots_ref.at[origin * fast + b]
            to_right(source, origin).wait_recv()

            @pl.when(a < slow - 1)
            def _():
                to_right(source, origin).start()

            for k in range(1, fast):
                to_fan(source, origin, k).start()

        @pl.when(a + step < slow)
        def _():
            origin = a + step
            source = slots_ref.at[origin * fast + b]
            to_left(source, origin).wait_recv()

            @pl.when(a > 0)
            def _():
                to_left(source, origin).start()

            for k in range(1, fast):
                to_fan(source, origin, k).start()

    for origin in range(slow):
        for k in range(1, fast):
            sender = lax.rem(b + k, fast)
            shard_copy(
                shard_ref, origin, sender, fan_sem.at[origin, k - 1], a * fast + sender
            ).wait_recv()
            to_fan(shard_ref, origin, k).wait_send()

        @pl.when((origin <= a) & (a < slow - 1))
        def _():
            to_right(shard_ref, origin).wait_send()

        @pl.when((origin >= a) & (a > 0))
        def _():
            to_left(shard_ref, origin).wait_send()

    for k in range(1, tp_count):
        peer_copy(k).wait()
    own_shard.wait()
    own_rows.wait()


def gathered(rows, shard, seq_count, tp_count):
    slow = 4 if seq_count % 4 == 0 else 1
    fast = seq_count // slow
    anywhere = pl.BlockSpec(memory_space=pl.ANY)
    dma = pltpu.SemaphoreType.DMA
    whole, slots = pl.pallas_call(
        functools.partial(gather_kernel, seq_count, tp_count),
        out_shape=[
            jax.ShapeDtypeStruct((rows.shape[0], rows.shape[1] * tp_count), rows.dtype),
            jax.ShapeDtypeStruct((seq_count,) + shard.shape, shard.dtype),
        ],
        in_specs=[anywhere, anywhere],
        out_specs=[anywhere, anywhere],
        scratch_shapes=[
            dma((2,)),
            dma((2, slow)),
            dma((slow, fast - 1)),
            dma((seq_count,)),
            dma((tp_count - 1,)),
            dma((tp_count - 1,)),
        ],
        compiler_params=pltpu.CompilerParams(
            collective_id=5, has_side_effects=True, vmem_limit_bytes=VMEM_BYTES
        ),
        name="gather_kernel",
    )(rows, shard)
    return whole, slots.reshape(seq_count * shard.shape[0], shard.shape[1])


def on_device(
    tokens,
    w_inner,
    w_states,
    w_step,
    conv_inner,
    conv_states,
    decay_rate,
    step_bias,
    skip_gain,
    norm_gain,
    w_output,
    block_owner,
    lengths,
):
    row_count = tokens.shape[0]
    local_blocks = row_count // BLOCK
    total_blocks = block_owner.shape[0]
    heads_here = w_step.shape[1]
    inner_here = w_inner.shape[2]
    state_size = w_states.shape[1] // 2
    head_size = inner_here // heads_here
    lag_rows = conv_inner.shape[0] - 1
    block_ids = jnp.arange(total_blocks, dtype=jnp.int32)
    same_owner = block_owner[:, None] == block_owner[None, :]
    first_block = jnp.min(jnp.where(same_owner, block_ids[None, :], total_blocks), axis=1)
    starting = (first_block == block_ids).astype(jnp.int32)
    request_ids = jnp.arange(lengths.shape[0], dtype=jnp.int32)
    own_length = jnp.sum(
        jnp.where(block_owner[:, None] == request_ids[None, :], lengths[None, :], 0), axis=1
    )
    valid_rows = jnp.clip(own_length - (block_ids - first_block) * BLOCK, 0, BLOCK)
    seq_index = lax.axis_index("seq")
    local_start = lax.dynamic_slice_in_dim(starting, seq_index * local_blocks, local_blocks)
    local_valid = lax.dynamic_slice_in_dim(valid_rows, seq_index * local_blocks, local_blocks)
    in_block = jnp.arange(row_count, dtype=jnp.int32) % BLOCK
    carry_on = jnp.repeat(local_start == 0, BLOCK)
    used = 2 * inner_here + 2 * state_size + heads_here
    filler = jnp.zeros((w_step.shape[0], -used % LANES), w_step.dtype)
    shard = jnp.concatenate(
        [w_inner.reshape(w_inner.shape[0], 2 * inner_here), w_states, w_step, filler], axis=1
    )
    whole, weights = gathered(tokens, shard, lax.axis_size("seq"), lax.axis_size("tp"))
    projected = jnp.dot(whole, weights, preferred_element_type=jnp.float32).astype(jnp.bfloat16)
    states_end = 2 * inner_here + 2 * state_size
    x_in = projected[:, inner_here : 2 * inner_here]
    bc_in = projected[:, 2 * inner_here : states_end]
    step_raw = projected[:, states_end : states_end + heads_here]
    edges = passed_along(projected[row_count - lag_rows :, inner_here:states_end], "seq", 1)
    edge_inner, edge_states = edges[:, :inner_here], edges[:, inner_here:]
    x_conv = convolve(x_in, edge_inner, conv_inner, in_block, carry_on)
    bc_conv = convolve(bc_in, edge_states, conv_states, in_block, carry_on)
    step_size = jax.nn.softplus(step_raw.astype(jnp.float32) + step_bias)
    log_decay = -decay_rate * step_size
    cumulative = jnp.cumsum(log_decay.reshape(local_blocks, BLOCK, heads_here), axis=1)
    final_log = cumulative[:, -1, :]
    keep_flag = jnp.where(local_start == 1, 0.0, 1.0).astype(jnp.float32)
    block_gain_each = jnp.exp(final_log) * keep_flag[:, None]
    gain_lanes = jnp.repeat(block_gain_each, head_size, axis=1)[:, None, :]
    keep_lanes = jnp.broadcast_to(keep_flag[:, None, None], gain_lanes.shape)
    cum_rows = cumulative.reshape(row_count, heads_here)
    by_rows = lambda width: pl.BlockSpec((BLOCK, width), lambda c: (c, 0))
    by_block = lambda *dims: pl.BlockSpec((1,) + dims, lambda c: (c, 0, 0))
    fixed = lambda *dims: pl.BlockSpec(dims, lambda c: (0, 0))
    turned = pl.BlockSpec((heads_here, BLOCK), lambda c: (0, c))
    params = pltpu.CompilerParams(vmem_limit_bytes=VMEM_BYTES)
    fresh, block_state = pl.pallas_call(
        functools.partial(state_kernel, head_size),
        grid=(local_blocks,),
        in_specs=[
            by_rows(inner_here),
            by_rows(2 * state_size),
            by_rows(heads_here),
            by_rows(heads_here),
            by_block(1, inner_here),
        ],
        out_specs=[by_block(state_size, inner_here), fixed(state_size, inner_here)],
        out_shape=[
            jax.ShapeDtypeStruct((local_blocks, state_size, inner_here), jnp.float32),
            jax.ShapeDtypeStruct((state_size, inner_here), jnp.float32),
        ],
        compiler_params=params,
        name="state_kernel",
    )(x_conv, bc_conv, cum_rows, step_size, gain_lanes)
    seq_count = lax.axis_size("seq")
    reach = min(seq_count - 1, -(-(total_blocks // 2) // local_blocks))
    device_gain = jnp.prod(gain_lanes, axis=0)
    gain_high = device_gain.astype(jnp.bfloat16)
    gain_low = (device_gain - gain_high.astype(jnp.float32)).astype(jnp.bfloat16)
    message = jnp.concatenate(
        [
            block_state.astype(jnp.bfloat16),
            jnp.broadcast_to(gain_high, (8, inner_here)),
            jnp.broadcast_to(gain_low, (8, inner_here)),
        ],
        axis=0,
    )
    entering = jnp.zeros((state_size, inner_here), jnp.float32)
    factor = jnp.ones((1, inner_here), jnp.float32)
    for distance in range(1, reach + 1):
        arrived = passed_along(message, "seq", distance).astype(jnp.float32)
        entering = entering + factor * arrived[:state_size]
        factor = factor * (
            arrived[state_size : state_size + 1] + arrived[state_size + 8 : state_size + 9]
        )
    normed, squares_here = pl.pallas_call(
        functools.partial(mix_kernel, head_size),
        grid=(local_blocks,),
        in_specs=[
            by_rows(inner_here),
            by_rows(2 * state_size),
            by_rows(inner_here),
            by_rows(heads_here),
            turned,
            turned,
            by_block(1, inner_here),
            by_block(1, inner_here),
            by_block(state_size, inner_here),
            fixed(state_size, inner_here),
            fixed(1, inner_here),
            fixed(1, inner_here),
        ],
        out_specs=[by_rows(inner_here), by_rows(1)],
        out_shape=[
            jax.ShapeDtypeStruct((row_count, inner_here), jnp.bfloat16),
            jax.ShapeDtypeStruct((row_count, 1), jnp.float32),
        ],
        scratch_shapes=[pltpu.VMEM((state_size, inner_here), jnp.float32)],
        compiler_params=params,
        name="mix_kernel",
    )(
        x_conv,
        bc_conv,
        projected,
        cum_rows,
        cum_rows.T,
        step_size.T,
        gain_lanes,
        keep_lanes,
        fresh,
        entering,
        jnp.repeat(skip_gain, head_size)[None, :],
        norm_gain[None, :],
    )
    tp_count = lax.axis_size("tp")
    squares = lax.psum(squares_here[:, 0], "tp")
    square_mean = squares / (inner_here * tp_count)
    summed = projected_sum(normed, lax.all_gather(w_output, "seq", axis=1, tiled=True), tp_count)
    summed = summed * lax.rsqrt(square_mean + 1e-05)[:, None]
    live = in_block < jnp.repeat(local_valid, BLOCK)
    return jnp.where(live[:, None], summed, 0.0).astype(jnp.bfloat16)


def solution(mesh):
    return jax.shard_map(
        on_device,
        mesh=mesh,
        in_specs=(
            P("seq", "tp"),
            P("seq", None, "tp"),
            P("seq", None),
            P("seq", "tp"),
            P(None, "tp"),
            P(),
            P("tp"),
            P("tp"),
            P("tp"),
            P("tp"),
            P("tp", "seq"),
            P(),
            P(),
        ),
        out_specs=P("seq", "tp"),
        check_vma=False,
    )
```
